32 devices in a mesh: seg: 4 (over x, core), sec: 8 (over z, y).
Axes of the slice: x: 2, y: 2, z: 4, core: 2. Of those that a mesh axis runs over, the one named last changes fastest.
Arguments:
- left_environment: bfloat16 [4, 64, 64, 1920], P('seg', 'sec'), may hold values from -0.125 to 0.125
- right_environment: bfloat16 [4, 64, 64, 1920], P('seg', 'sec'), may hold values from -0.75 to 0.75
- site_previous: bfloat16 [4, 64, 64, 256], P('seg', 'sec'), may hold values from -0.75 to 0.75
- state_start: float32 [4, 64, 64, 256], P('seg', 'sec'), may hold values from -36 to 36
- preconditioner: float32 [4, 64, 64, 256], P('seg', 'sec'), may hold values from 0.25 to 4
- channel_tensor: bfloat16 [30, 4, 30, 4], replicated, may hold values from -0.5 to 0.5
- channel_mask: int32 [30, 30], replicated, may hold values 0 or 1
- sector_shift: int32 [5, 64], replicated, may hold values from 0 to 63, as said below
- left_sizes: int32 [64], replicated, may hold values from 32 to 64, as said below
- right_sizes: int32 [64, 4], replicated, may hold values from 32 to 64, as said below
Outputs:
- bond_state: float32 [4, 64, 64, 256], P('seg', 'sec')
- energy: float32 [4], P('seg')
The draws below stay inside these ranges and needn't reach their ends.
Inputs may be any that keep to these rules, and one draw needn't show every extreme that they name: Each row is a permutation of the 64 sectors; for every group of 8 consecutive sectors and every other such group, at most 5 pairs of a class k and a sector l of the first group have sector_shift[k, l] in the second group, and some pair of groups reaches 5. `left_sizes`: some sector fills its tile and some has 32 live states. `right_sizes`: some block fills its tile and some has 32 live states.
All inputs are finite; a program needn't handle non-finite values.
Results may differ from the reference program's by a relative error of at most 0.012.
Values may be sent and summed in bfloat16 or wider, within the bound.
A program may use at most 256 MiB of HBM per device.

```python
import jax
import jax.numpy as jnp
from jax import lax

W = 30
D = 4
B = 64
SEC_DEV = 8
CLASSES = 5
ITERS = 2
SECTORS = 64
SEGS = 4
N_SEC = 8


def sizes_with_ends(key, entries):
    first_key, second_key, third_key = jax.random.split(key, 3)
    values = jax.random.randint(first_key, (entries,), B // 2, B + 1)
    top_place = jax.random.randint(second_key, (), 0, entries)
    low_place = (top_place + 1 + jax.random.randint(third_key, (), 0, entries - 1)) % entries
    positions = jnp.arange(entries)
    values = jnp.where(positions == low_place, B // 2, values)
    values = jnp.where(positions == top_place, B, values)
    return values.astype(jnp.int32)


def draw_left_sizes(key, part):
    return sizes_with_ends(jax.random.fold_in(key, 11), SECTORS)


def draw_right_sizes(key, part):
    return sizes_with_ends(jax.random.fold_in(key, 23), SECTORS * D).reshape(SECTORS, D)


def draw_sector_shift(key, part):
    group_count = SECTORS // SEC_DEV
    first_key, second_key = jax.random.split(jax.random.fold_in(key, 37))
    relabel = jax.random.permutation(first_key, group_count)
    slot_keys = jax.random.split(second_key, CLASSES * group_count)
    slot_order = jax.vmap(lambda one_key: jax.random.permutation(one_key, SEC_DEV))(slot_keys)
    slot_order = slot_order.reshape(CLASSES, group_count, SEC_DEV)
    sector = jnp.arange(SECTORS, dtype=jnp.int32)
    group = sector // SEC_DEV
    local = sector % SEC_DEV
    charge = jnp.arange(CLASSES, dtype=jnp.int32)[:, None]
    raw_owner = (group[None, :] + charge * SEC_DEV + local[None, :]) % group_count
    owner = relabel[raw_owner]
    slot = slot_order[charge, owner, local[None, :]]
    return (owner * SEC_DEV + slot).astype(jnp.int32)


def sector_ramp(top):
    fraction = jnp.arange(SECTORS, dtype=jnp.float32) / float(SECTORS - 1)
    return jnp.exp(jnp.log(top) * fraction)[None, :, None, None]


def draw_state_start(key, part):
    shape = (SEGS, SECTORS, B, D * B)
    inner_key = jax.random.fold_in(key, 51)
    base = jnp.clip(jax.random.normal(inner_key, shape, jnp.float32), -6.0, 6.0)
    return base * sector_ramp(6.0)


def draw_preconditioner(key, part):
    shape = (SEGS, SECTORS, B, D * B)
    inner_key = jax.random.fold_in(key, 67)
    base = jnp.exp(jax.random.uniform(inner_key, shape, jnp.float32, jnp.log(0.25), 0.0))
    return base * sector_ramp(4.0)


def set_ends(drawn, stream_key, least, high):
    index_at = [jax.random.randint(jax.random.fold_in(stream_key, axis), (), 0, length) for axis, length in enumerate(drawn.shape)]
    main_axis = drawn.shape.index(max(drawn.shape))
    next_to = index_at[:main_axis] + [(index_at[main_axis] + 1) % drawn.shape[main_axis]] + index_at[main_axis + 1:]
    return drawn.at[tuple(index_at)].set(least).at[tuple(next_to)].set(high)


def block_scale(own_key, dims, pieces, smallest, high):
    loudness, own = 1.0, jax.random.fold_in(own_key, 6)
    for axis_at, blocks in pieces:
        draws = jnp.exp(jax.random.uniform(jax.random.fold_in(own, axis_at), (blocks,), jnp.float32, smallest / len(pieces), high / len(pieces)))
        loudness = loudness * jnp.repeat(draws, dims[axis_at] // blocks).reshape([-1 if axis == axis_at else 1 for axis in range(len(dims))])
    return loudness


def gaussian(key, shape, deviation, bound, shards=(), held_as=jnp.bfloat16):
    values = deviation * jax.random.normal(key, shape, jnp.float32)
    if shards:
        values = values * block_scale(key, shape, shards, -0.22, 0.18)
    return jnp.clip(values, -bound, bound).astype(held_as)


def setup_inputs(seed: int = 0) -> dict:
    streams_of = jax.random.split(jax.random.key(seed), 11)
    return {
        "left_environment": gaussian(streams_of[0], (SEGS, SECTORS, B, W * B), (W * B) ** -0.5, 0.125, ((0, 4), (1, 8))),
        "right_environment": gaussian(streams_of[1], (SEGS, SECTORS, B, W * B), B ** -0.5, 0.75, ((0, 4), (1, 8))),
        "site_previous": gaussian(streams_of[2], (SEGS, SECTORS, B, D * B), B ** -0.5, 0.75, ((0, 4), (1, 8))),
        "state_start": draw_state_start(jax.random.fold_in(streams_of[10], 71), 0),
        "preconditioner": draw_preconditioner(jax.random.fold_in(streams_of[10], 71), 0),
        "channel_tensor": gaussian(streams_of[5], (W, D, W, D), (W * D) ** -0.5, 0.5),
        "channel_mask": set_ends((jax.random.randint(streams_of[6], (W, W), 0, 2) < 1).astype(jnp.int32), jax.random.fold_in(streams_of[6], 1), 0, 1),
        "sector_shift": draw_sector_shift(jax.random.fold_in(streams_of[10], 71), 0),
        "left_sizes": draw_left_sizes(jax.random.fold_in(streams_of[10], 71), 0),
        "right_sizes": draw_right_sizes(jax.random.fold_in(streams_of[10], 71), 0),
    }


EPSILON = 1e-06
HIGHEST_PRECISION = lax.Precision.HIGHEST

def live_masks(left_sizes, right_sizes):
    row_live = jnp.arange(B, dtype=jnp.int32)[None, :] < left_sizes[:, None]
    column_live = jnp.arange(B, dtype=jnp.int32)[None, None, :] < right_sizes[:, :, None]
    joined_live = row_live[:, :, None, None] & column_live[:, None, :, :]
    return joined_live.astype(jnp.float32).reshape(SECTORS, B, D * B)

def build_environment(environment, site_blocks, channel_mix, sector_shift):
    groups = W // CLASSES
    split_left = environment.astype(jnp.float32).reshape(SECTORS, B, CLASSES, groups, B)
    tensor = site_blocks.astype(jnp.float32).reshape(SECTORS, B, D, B)
    contracted = jnp.einsum('lpkja,lasb->lpkjsb', split_left, tensor, precision=HIGHEST_PRECISION).astype(jnp.bfloat16)
    channel_split = channel_mix.reshape(CLASSES, groups, D, W, D)
    accumulated = jnp.zeros((SECTORS, B, W, B), jnp.float32)
    for charge in range(CLASSES):
        shifted_site = jnp.take(tensor, sector_shift[charge], axis=0)
        carried = jnp.einsum('jtvs,lpjsb->lptvb', channel_split[charge], contracted[:, :, charge].astype(jnp.float32), precision=HIGHEST_PRECISION).astype(jnp.bfloat16)
        accumulated = accumulated + jnp.einsum('lpte,lptvb->levb', shifted_site, carried.astype(jnp.float32), precision=HIGHEST_PRECISION)
    return accumulated.astype(jnp.bfloat16).reshape(SECTORS, B, W * B)

def apply_operator(vector_low, left_split, right_split, channel_mix, sector_shift, live_mask):
    blocks = vector_low.astype(jnp.float32).reshape(SECTORS, B, D, B)
    right_product = jnp.einsum('lasb,lbvc->lasvc', blocks, right_split, precision=HIGHEST_PRECISION).astype(jnp.bfloat16)
    mixed_product = jnp.einsum('wtvs,lasvc->lwatc', channel_mix, right_product.astype(jnp.float32), precision=HIGHEST_PRECISION).astype(jnp.bfloat16)
    grouped = mixed_product.astype(jnp.float32).reshape(SECTORS, CLASSES, W // CLASSES, B, D, B)
    partial_value = jnp.einsum('lpkja,lkjatc->lkptc', left_split, grouped, precision=HIGHEST_PRECISION)
    partial_value = partial_value.reshape(N_SEC, SEC_DEV, CLASSES, B * D * B)
    onehot = (sector_shift[:, :, None] == jnp.arange(SECTORS, dtype=jnp.int32)[None, None, :]).astype(jnp.float32)
    onehot = onehot.reshape(CLASSES, N_SEC, SEC_DEV, SECTORS)
    group_sums = jnp.einsum('kgim,gikx->gmx', onehot, partial_value, precision=HIGHEST_PRECISION)
    rounded = lax.optimization_barrier(group_sums.astype(jnp.bfloat16)).astype(jnp.float32)
    return live_mask * lax.optimization_barrier(jnp.sum(rounded, axis=0)).reshape(SECTORS, B, D * B)

def reference(left_environment, right_environment, site_previous, state_start, preconditioner, channel_tensor, channel_mask, sector_shift, left_sizes, right_sizes):
    channel_mix = channel_tensor.astype(jnp.float32) * channel_mask.astype(jnp.float32)[:, None, :, None]
    live_mask = live_masks(left_sizes, right_sizes)

    def solve_segment(segment):
        before = jnp.maximum(segment - 1, 0).astype(jnp.int32)
        following = jnp.minimum(segment + 1, SEGS - 1).astype(jnp.int32)
        handed = build_environment(left_environment[before], site_previous[before], channel_mix, sector_shift)
        left_used = jnp.where(segment == 0, left_environment[segment], handed)
        right_used = right_environment[following]
        left_split = left_used.astype(jnp.float32).reshape(SECTORS, B, CLASSES, W // CLASSES, B)
        right_split = right_used.astype(jnp.float32).reshape(SECTORS, B, W, B)
        entries = float(SECTORS * B * D * B)

        def inner(vector_one, vector_two):
            return jnp.sum(vector_one * vector_two) / entries

        def operator(vector):
            return apply_operator(vector.astype(jnp.bfloat16), left_split, right_split, channel_mix, sector_shift, live_mask)
        current = live_mask * state_start[segment]
        current = current / jnp.sqrt(inner(current, current) + EPSILON)
        applied = operator(current)
        precondition = preconditioner[segment]
        for iteration in range(ITERS):
            rayleigh_value = inner(current, applied)
            correction = precondition * (applied - rayleigh_value * current)
            correction = correction - inner(current, correction) * current
            direction = correction / jnp.sqrt(inner(correction, correction) + EPSILON)
            product = operator(direction)
            cross_term = 0.5 * (inner(current, product) + inner(direction, applied))
            far_term = inner(direction, product)
            rotation = 0.5 * jnp.arctan2(-2.0 * cross_term, far_term - rayleigh_value)
            current = jnp.cos(rotation) * current + jnp.sin(rotation) * direction
            applied = jnp.cos(rotation) * applied + jnp.sin(rotation) * product
        return (current, inner(current, applied))
    bond_state, energy = lax.map(solve_segment, jnp.arange(SEGS, dtype=jnp.int32))
    return (bond_state, energy)
```

```python
import functools

import jax
import jax.numpy as jnp
from jax import lax
from jax.experimental import pallas as pl
from jax.experimental.pallas import tpu as pltpu
from jax.sharding import PartitionSpec as P

W = 30
D = 4
B = 64
SEC_DEV = 8
CLASSES = 5
ITERS = 2


EPSILON = 1e-06
HIGHEST_PRECISION = lax.Precision.HIGHEST


def passed_along(block, axis, distance):
    devices = range(lax.axis_size(axis))
    route = [(i - distance, i) for i in devices if i - distance in devices]
    return lax.ppermute(block, axis, route)


def live_masks(left_sizes, right_sizes, offset):
    row_limit = lax.dynamic_slice_in_dim(left_sizes, offset, SEC_DEV, 0)
    column_limit = lax.dynamic_slice_in_dim(right_sizes, offset, SEC_DEV, 0)
    row_live = jnp.arange(B, dtype=jnp.int32)[None, :] < row_limit[:, None]
    column_live = jnp.arange(B, dtype=jnp.int32)[None, None, :] < column_limit[:, :, None]
    joined_live = row_live[:, :, None, None] & column_live[:, None, :, :]
    return joined_live.astype(jnp.float32).reshape(SEC_DEV, B, D * B)


def send_order(group_total):
    return sorted(range(1, group_total), key=lambda step: -min(step, group_total - step))


def pair_tables(sector_shift, group, group_total):
    target_list = lax.dynamic_slice_in_dim(sector_shift, group * SEC_DEV, SEC_DEV, 1).T.reshape(
        SEC_DEV * CLASSES
    )
    steps = send_order(group_total)
    place_of = [group_total - 1] * group_total
    for place, step in enumerate(steps):
        place_of[step] = place
    place_of = jnp.array(place_of, dtype=jnp.int32)
    step_list = (target_list // SEC_DEV - group + group_total) % group_total
    one_hot = step_list[:, None] == jnp.arange(group_total, dtype=jnp.int32)[None, :]
    place_list = jnp.sum(jnp.where(one_hot, place_of[None, :], 0), axis=1)
    order = jnp.arange(SEC_DEV * CLASSES, dtype=jnp.int32)
    sort_key = place_list * (SEC_DEV * CLASSES) + order
    position = jnp.sum((sort_key[None, :] < sort_key[:, None]).astype(jnp.int32), axis=1)
    place_start = jnp.sum(
        (place_list[:, None] < jnp.arange(group_total, dtype=jnp.int32)[None, :]).astype(jnp.int32), axis=0
    )
    own_start = jnp.sum((place_list[None, :] < place_list[:, None]).astype(jnp.int32), axis=1)
    return target_list, place_list, position, place_start, position - own_start


def routing_tables(sector_shift, my_group, group_total, capacity):
    pairs = SEC_DEV * CLASSES
    groups = jnp.arange(group_total, dtype=jnp.int32)
    targets, places, positions, starts, ranks = jax.vmap(
        lambda group: pair_tables(sector_shift, group, group_total)
    )(groups)
    mine = groups == my_group
    my_position = jnp.sum(jnp.where(mine[:, None], positions, 0), axis=0)
    my_start = jnp.sum(jnp.where(mine[:, None], starts, 0), axis=0)
    index = jnp.arange(pairs, dtype=jnp.int32)
    sorted_pair = jnp.sum(jnp.where(my_position[None, :] == index[:, None], index[None, :], 0), axis=1)
    slot_source = (
        my_start[: group_total - 1, None] + jnp.arange(capacity, dtype=jnp.int32)[None, :]
    ).reshape(-1)
    slot_source = jnp.minimum(slot_source, pairs - 1)
    local = targets - my_group * SEC_DEV
    slots = (group_total - 1) * capacity
    value = jnp.where(mine[:, None], slots + positions, places * capacity + ranks)
    wanted = jnp.arange(SEC_DEV, dtype=jnp.int32)
    class_of = index % CLASSES
    hit = (local[None, None, :, :] == wanted[:, None, None, None]) & (
        class_of[None, None, None, :] == jnp.arange(CLASSES, dtype=jnp.int32)[None, :, None, None]
    )
    source = jnp.sum(jnp.where(hit, value[None, None], 0), axis=(2, 3)).reshape(pairs)
    from_self = (source >= slots).astype(jnp.int32)
    arrived_slot = jnp.where(from_self == 1, 0, source)
    own_position = jnp.where(from_self == 1, source - slots, 0)
    return sorted_pair, slot_source, from_self, arrived_slot, own_position


def gate_kernel(mix_ref, right_ref, gate_ref, spread):
    sites, channel_sites, _ = mix_ref.shape
    classes = gate_ref.shape[0]
    halves = right_ref.shape[2] // 128
    bond = 2 * halves
    per_class = channel_sites // classes
    low_lanes = lax.broadcasted_iota(jnp.int32, (halves, 128), 1) < 64
    for site in range(sites):
        mixed = jnp.dot(mix_ref[site], right_ref[0], preferred_element_type=jnp.float32)
        for half in range(halves):
            spread[half * channel_sites : (half + 1) * channel_sites, :] = mixed[
                :, half * 128 : (half + 1) * 128
            ]

        def one_class(charge, carry):
            for pair in range(per_class // 2):
                first = charge * per_class + 2 * pair
                one = spread[pl.ds(first, halves, stride=channel_sites), :]
                two = spread[pl.ds(first + 1, halves, stride=channel_sites), :]
                upper = jnp.where(low_lanes, one, pltpu.roll(two, 64, 1))
                lower = jnp.where(low_lanes, pltpu.roll(one, 64, 1), two)
                lanes = slice(pair * 128, (pair + 1) * 128)
                gate_ref[charge, site * bond : site * bond + halves, lanes] = upper.astype(jnp.bfloat16)
                gate_ref[charge, site * bond + halves : (site + 1) * bond, lanes] = lower.astype(
                    jnp.bfloat16
                )
            return carry

        lax.fori_loop(0, classes, one_class, 0)


def environment_kernel(shift_ref, mix_ref, left_ref, site_ref, every_ref, out_ref, spread, turned):
    classes, bond, per_columns = out_ref.shape
    per_class = per_columns // bond
    mixed_rows = mix_ref.shape[0]
    sites = every_ref.shape[2] // bond
    channels = classes * per_class
    halves = bond // 2
    sector = pl.program_id(0)
    sectors = pl.num_programs(0)
    low_lanes = lax.broadcasted_iota(jnp.int32, (halves, 128), 1) < 64
    for charge in range(classes):
        shifted = every_ref[shift_ref[charge * sectors + sector]]
        joined = lax.dot_general(
            shifted,
            left_ref[0, :, charge * per_columns : (charge + 1) * per_columns],
            (((0,), (0,)), ((), ())),
            preferred_element_type=jnp.float32,
        )
        for site in range(sites):
            for pair in range(per_class // 2):
                lanes = slice(pair * 128, (pair + 1) * 128)
                one = joined[site * bond : site * bond + halves, lanes]
                two = joined[site * bond + halves : (site + 1) * bond, lanes]
                row = (charge * per_class + 2 * pair) * sites + site
                spread[pl.ds(row, halves, stride=mixed_rows), :] = jnp.where(
                    low_lanes, one, pltpu.roll(two, 64, 1)
                )
                spread[pl.ds(row + sites, halves, stride=mixed_rows), :] = jnp.where(
                    low_lanes, pltpu.roll(one, 64, 1), two
                )

    def mix_two(half, carry):
        base = pl.multiple_of(half * 2 * mixed_rows, 8)
        after = pl.multiple_of(base + mixed_rows, 8)
        both = jnp.concatenate(
            [spread[pl.ds(base, mixed_rows), :], spread[pl.ds(after, mixed_rows), :]], axis=1
        ).astype(jnp.bfloat16)
        mixed = jnp.dot(mix_ref[...], both, preferred_element_type=jnp.float32)
        spread[pl.ds(base, mixed_rows), :] = mixed[:, :128]
        spread[pl.ds(after, mixed_rows), :] = mixed[:, 128:]
        return carry

    lax.fori_loop(0, halves // 2, mix_two, 0, unroll=4)
    for channel in range(channels):
        for pair in range(sites // 2):
            row = channel * sites + 2 * pair
            one = spread[pl.ds(row, halves, stride=mixed_rows), :]
            two = spread[pl.ds(row + 1, halves, stride=mixed_rows), :]
            lanes = slice(pair * 128, (pair + 1) * 128)
            turned[channel * bond : channel * bond + halves, lanes] = jnp.where(
                low_lanes, one, pltpu.roll(two, 64, 1)
            ).astype(jnp.bfloat16)
            turned[channel * bond + halves : (channel + 1) * bond, lanes] = jnp.where(
                low_lanes, pltpu.roll(one, 64, 1), two
            ).astype(jnp.bfloat16)
    for charge in range(classes):
        rows = slice(charge * per_columns, (charge + 1) * per_columns)
        built = jnp.dot(turned[rows, :], site_ref[0], preferred_element_type=jnp.float32)
        for pair in range(per_class // 2):
            one = built[2 * pair * bond : (2 * pair + 1) * bond]
            two = built[(2 * pair + 1) * bond : (2 * pair + 2) * bond]
            out_ref[charge, :, pair * 128 : (pair + 1) * 128] = jnp.concatenate(
                [one, two], axis=1
            ).astype(jnp.bfloat16)


def build_environment(environment, site_blocks, channel_mix, sector_shift, offset):
    every_site = lax.all_gather(site_blocks, "sec", axis=0, tiled=True)
    sectors = environment.shape[0]
    targets = lax.dynamic_slice_in_dim(sector_shift, offset, sectors, 1).reshape(-1)
    mix = channel_mix.transpose(2, 3, 0, 1).reshape(W * D, W * D)
    own = site_blocks.reshape(sectors, B, D, B).transpose(0, 2, 1, 3).reshape(sectors, D * B, B)
    per_columns = W // CLASSES * B
    return pl.pallas_call(
        environment_kernel,
        grid=(sectors,),
        in_specs=[
            pl.BlockSpec(memory_space=pltpu.SMEM),
            pl.BlockSpec((W * D, W * D), lambda sector: (0, 0)),
            pl.BlockSpec((1, B, W * B), lambda sector: (sector, 0, 0)),
            pl.BlockSpec((1, D * B, B), lambda sector: (sector, 0, 0)),
            pl.BlockSpec(every_site.shape, lambda sector: (0, 0, 0)),
        ],
        out_specs=pl.BlockSpec((CLASSES, B, per_columns), lambda sector: (sector, 0, 0)),
        out_shape=jax.ShapeDtypeStruct((sectors * CLASSES, B, per_columns), jnp.bfloat16),
        scratch_shapes=[
            pltpu.VMEM((B // 2 * W * D, 2 * B), jnp.float32),
            pltpu.VMEM((W * B, D * B), jnp.bfloat16),
        ],
        compiler_params=pltpu.CompilerParams(vmem_limit_bytes=32 * 1024 * 1024),
        cost_estimate=pl.CostEstimate(
            flops=8 * sectors * W * D * W * D * B * B, bytes_accessed=6000000, transcendentals=0
        ),
    )(targets, mix, environment, own, every_site)


def build_gate(right_used, channel_mix):
    sectors = right_used.shape[0]
    halves = B // 2
    right_split = right_used.reshape(sectors, 2, halves, W, B).transpose(0, 3, 2, 1, 4)
    right_split = right_split.reshape(sectors, W, B * B)
    mix = channel_mix.transpose(3, 0, 1, 2).reshape(D, W * D, W)
    shape = (sectors * CLASSES, D * B, W // CLASSES * D * B)
    return pl.pallas_call(
        gate_kernel,
        grid=(sectors,),
        in_specs=[
            pl.BlockSpec((D, W * D, W), lambda sector: (0, 0, 0)),
            pl.BlockSpec((1, W, B * B), lambda sector: (sector, 0, 0)),
        ],
        out_specs=pl.BlockSpec((CLASSES,) + shape[1:], lambda sector: (sector, 0, 0)),
        out_shape=jax.ShapeDtypeStruct(shape, jnp.bfloat16),
        scratch_shapes=[pltpu.VMEM((halves * W * D, 2 * B), jnp.float32)],
        compiler_params=pltpu.CompilerParams(vmem_limit_bytes=32 * 1024 * 1024),
        cost_estimate=pl.CostEstimate(
            flops=2 * sectors * D * W * D * W * B * B, bytes_accessed=36000000, transcendentals=0
        ),
    )(mix, right_split)


def davidson_kernel(
    n,
    capacity,
    total_entries,
    pair_ref,
    slot_ref,
    self_ref,
    arrived_ref,
    own_ref,
    mask_ref,
    start_ref,
    precondition_ref,
    left_ref,
    gate_ref,
    state_ref,
    energy_ref,
    current,
    applied,
    direction,
    product,
    low,
    stacked,
    partial,
    outgoing,
    incoming,
    row_send,
    row_all,
    send_sem,
    recv_sem,
    row_send_sem,
    row_recv_sem,
):
    pairs = left_ref.shape[0]
    sectors, rows, columns = current.shape
    classes = pairs // sectors
    channels = left_ref.shape[2] // rows
    steps = send_order(n)
    me = lax.axis_index("sec")

    barrier = pltpu.get_barrier_semaphore()
    for step in steps:
        pl.semaphore_signal(
            barrier,
            inc=1,
            device_id={"sec": lax.rem(me + step, n)},
            device_id_type=pl.DeviceIdType.MESH,
        )
    pl.semaphore_wait(barrier, n - 1)

    def fold(values):
        eight = jnp.sum(values.reshape(rows // 8, 8, columns), axis=0)
        return eight[:, : columns // 2] + eight[:, columns // 2 :]

    def all_sums(turn, count, products):
        zero = jnp.zeros((8, columns // 2), jnp.float32)

        def body(sector, sums):
            return tuple(total + fold(term) for total, term in zip(sums, products(sector)))

        sums = lax.fori_loop(0, sectors, body, (zero,) * count)
        for entry in range(8):
            if entry < count:
                row_send[turn, entry : entry + 1, :] = jnp.sum(sums[entry], axis=0, keepdims=True)
            else:
                row_send[turn, entry : entry + 1, :] = zero[0:1]
        copies = []
        for place, step in enumerate(steps):
            copies.append(
                pltpu.make_async_remote_copy(
                    src_ref=row_send.at[turn],
                    dst_ref=row_all.at[turn, me],
                    send_sem=row_send_sem.at[turn, place],
                    recv_sem=row_recv_sem.at[turn, place],
                    device_id={"sec": lax.rem(me + step, n)},
                    device_id_type=pl.DeviceIdType.MESH,
                )
            )
            copies[-1].start()
        row_all[turn, me] = row_send[turn]
        for copy in copies:
            copy.wait()
        whole = row_all[turn, 0]
        for group in range(1, n):
            whole = whole + row_all[turn, group]
        whole = jnp.sum(whole, axis=1, keepdims=True) / total_entries
        return [whole[entry : entry + 1, :] for entry in range(count)]

    def operator(turn, result):
        def one_pair(position, carry):
            pair = pair_ref[position]
            sector = pair_ref[pairs + position]
            mixed = jnp.dot(low[sector], gate_ref[pair], preferred_element_type=jnp.float32)
            for channel in range(channels):
                stacked[channel * rows : (channel + 1) * rows, :] = mixed[
                    :, channel * columns : (channel + 1) * columns
                ].astype(jnp.bfloat16)
            partial[position] = jnp.dot(
                left_ref[pair], stacked[...], preferred_element_type=jnp.float32
            )
            return carry

        copies = []
        done = 0
        for place, step in enumerate(steps):
            upto = min((place + 1) * capacity, pairs)
            lax.fori_loop(done, upto, one_pair, 0)
            done = upto
            for rank in range(capacity):
                outgoing[turn, place, rank] = partial[slot_ref[place * capacity + rank]].astype(
                    jnp.bfloat16
                )
            copies.append(
                pltpu.make_async_remote_copy(
                    src_ref=outgoing.at[turn, place],
                    dst_ref=incoming.at[turn, place],
                    send_sem=send_sem.at[turn, place],
                    recv_sem=recv_sem.at[turn, place],
                    device_id={"sec": lax.rem(me + step, n)},
                    device_id_type=pl.DeviceIdType.MESH,
                )
            )
            copies[-1].start()
        if done < pairs:
            lax.fori_loop(done, pairs, one_pair, 0)
        for copy in copies:
            copy.wait()
        landed = incoming.at[turn]

        def gather(sector, carry):
            total = jnp.zeros((rows, columns), jnp.float32)
            for charge in range(classes):
                entry = sector * classes + charge
                slot = arrived_ref[entry]
                came = landed[arrived_ref[pairs + entry], slot].astype(jnp.float32)
                own = partial[own_ref[entry]]
                own_part = jnp.broadcast_to(self_ref[entry], (rows, columns)) == 1
                total = total + jnp.where(own_part, own, came)
            result[sector] = mask_ref[sector] * total
            return carry

        lax.fori_loop(0, sectors, gather, 0)

    def first(sector, carry):
        current[sector] = mask_ref[sector] * start_ref[sector]
        return carry

    lax.fori_loop(0, sectors, first, 0)
    (start_square,) = all_sums(0, 1, lambda s: (current[s] * current[s],))
    start_scale = 1.0 / jnp.sqrt(start_square + EPSILON)

    def normalise(sector, carry):
        value = current[sector] * start_scale
        current[sector] = value
        low[sector] = value.astype(jnp.bfloat16)
        return carry

    lax.fori_loop(0, sectors, normalise, 0)
    operator(0, applied)
    energy = None
    for iteration in range(ITERS):

        def shaped(sector):
            one, two = current[sector], applied[sector]
            weight = precondition_ref[sector]
            weighted_one, weighted_two = weight * one, weight * two
            return (
                one * two,
                one * one,
                one * weighted_two,
                one * weighted_one,
                weighted_two * weighted_two,
                weighted_two * weighted_one,
                weighted_one * weighted_one,
            )

        sums = all_sums(1 + 2 * iteration, 7, shaped)
        rho = sums[0]
        correlation = sums[2] - rho * sums[3]
        square = sums[4] - 2.0 * rho * sums[5] + rho * rho * sums[6]
        square = square - 2.0 * correlation * correlation + correlation * correlation * sums[1]
        scale = 1.0 / jnp.sqrt(jnp.maximum(square, 0.0) + EPSILON)

        def correct(sector, carry):
            one = current[sector]
            value = precondition_ref[sector] * (applied[sector] - rho * one)
            value = (value - correlation * one) * scale
            direction[sector] = value
            low[sector] = value.astype(jnp.bfloat16)
            return carry

        lax.fori_loop(0, sectors, correct, 0)
        operator(1 + iteration, product)
        sums = all_sums(
            2 + 2 * iteration,
            3,
            lambda s: (current[s] * product[s], direction[s] * applied[s], direction[s] * product[s]),
        )
        cross = 0.5 * (sums[0] + sums[1])
        far = sums[2]
        across, along = -2.0 * cross, far - rho
        largest = jnp.maximum(jnp.abs(across), jnp.abs(along))
        still = largest == 0.0
        safe = jnp.where(still, 1.0, largest)
        across, along = across / safe, jnp.where(still, 1.0, along / safe)
        length = jnp.sqrt(across * across + along * along)
        bigger = jnp.sqrt(0.5 * (length + jnp.abs(along)) / length)
        smaller = 0.5 * jnp.abs(across) / (length * bigger)
        ahead = along >= 0.0
        cosine = jnp.where(ahead, bigger, smaller)
        sine = jnp.where(ahead, smaller, bigger)
        sine = jnp.where(across > 0.0, sine, -sine)
        energy = cosine * cosine * rho + 2.0 * cosine * sine * cross + sine * sine * far
        last = iteration == ITERS - 1

        def rotate(sector, carry):
            value = cosine * current[sector] + sine * direction[sector]
            if last:
                state_ref[sector] = value
            else:
                current[sector] = value
                applied[sector] = cosine * applied[sector] + sine * product[sector]
            return carry

        lax.fori_loop(0, sectors, rotate, 0)
    energy_ref[...] = jnp.broadcast_to(energy, energy_ref.shape)


def davidson(tables, live_mask, start, precondition, left_pairs, gate, group_total, capacity):
    pairs = left_pairs.shape[0]
    sectors, rows, columns = start.shape
    sorted_pair, slot_source, from_self, arrived_slot, own_position = tables
    sorted_pair = jnp.concatenate([sorted_pair, sorted_pair // CLASSES])
    arrived_slot = jnp.concatenate([arrived_slot % capacity, arrived_slot // capacity])
    turns = ITERS + 1
    rounds = 2 * ITERS + 1
    others = group_total - 1
    smem = pl.BlockSpec(memory_space=pltpu.SMEM)
    vmem = pl.BlockSpec(memory_space=pltpu.VMEM)
    vector = pltpu.VMEM((sectors, rows, columns), jnp.float32)
    kernel = functools.partial(
        davidson_kernel, group_total, capacity, float(group_total * sectors * rows * columns)
    )
    return pl.pallas_call(
        kernel,
        out_shape=(
            jax.ShapeDtypeStruct(start.shape, jnp.float32),
            jax.ShapeDtypeStruct((8, 128), jnp.float32),
        ),
        in_specs=[smem] * 5 + [vmem] * 5,
        out_specs=(vmem, vmem),
        scratch_shapes=[
            vector,
            vector,
            vector,
            vector,
            pltpu.VMEM((sectors, rows, columns), jnp.bfloat16),
            pltpu.VMEM((left_pairs.shape[2], columns), jnp.bfloat16),
            pltpu.VMEM((pairs, rows, columns), jnp.float32),
            pltpu.VMEM((turns, others, capacity, rows, columns), jnp.bfloat16),
            pltpu.VMEM((turns, others, capacity, rows, columns), jnp.bfloat16),
            pltpu.VMEM((rounds, 8, columns // 2), jnp.float32),
            pltpu.VMEM((rounds, group_total, 8, columns // 2), jnp.float32),
            pltpu.SemaphoreType.DMA((turns, others)),
            pltpu.SemaphoreType.DMA((turns, others)),
            pltpu.SemaphoreType.DMA((rounds, others)),
            pltpu.SemaphoreType.DMA((rounds, others)),
        ],
        compiler_params=pltpu.CompilerParams(
            collective_id=0, has_side_effects=True, vmem_limit_bytes=58 * 1024 * 1024
        ),
    )(
        sorted_pair,
        slot_source,
        from_self,
        arrived_slot,
        own_position,
        live_mask,
        start,
        precondition,
        left_pairs,
        gate,
    )


def on_device(
    left_environment,
    right_environment,
    site_previous,
    state_start,
    preconditioner,
    channel_tensor,
    channel_mask,
    sector_shift,
    left_sizes,
    right_sizes,
):
    group_total = lax.axis_size("sec")
    my_group = lax.axis_index("sec")
    offset = my_group * SEC_DEV
    capacity = (CLASSES * SEC_DEV + group_total - 1) // group_total
    channel_mix = channel_tensor * channel_mask.astype(jnp.bfloat16)[:, None, :, None]
    live_mask = live_masks(left_sizes, right_sizes, offset)
    own_left = left_environment[0]
    position = lax.axis_index("seg")
    came_right = passed_along(right_environment[0], "seg", -1)
    right_used = jnp.where(position == lax.axis_size("seg") - 1, right_environment[0], came_right)
    fresh = build_environment(own_left, site_previous[0], channel_mix, sector_shift, offset)
    handed = passed_along(fresh, "seg", 1)
    own_pairs = (
        own_left.reshape(SEC_DEV, B, CLASSES, W // CLASSES * B)
        .transpose(0, 2, 1, 3)
        .reshape(SEC_DEV * CLASSES, B, W // CLASSES * B)
    )
    left_pairs = jnp.where(position == 0, own_pairs, handed)
    gate = build_gate(right_used, channel_mix)
    tables = routing_tables(sector_shift, my_group, group_total, capacity)
    state, energy = davidson(
        tables, live_mask, state_start[0], preconditioner[0], left_pairs, gate, group_total, capacity
    )
    return (state[None], energy[0, 0:1])


def solution(mesh):
    in_specs = (
        P("seg", "sec", None, None),
        P("seg", "sec", None, None),
        P("seg", "sec", None, None),
        P("seg", "sec", None, None),
        P("seg", "sec", None, None),
        P(),
        P(),
        P(),
        P(),
        P(),
    )
    out_specs = (P("seg", "sec", None, None), P("seg"))
    return jax.shard_map(
        on_device, mesh=mesh, in_specs=in_specs, out_specs=out_specs, check_vma=False
    )
```

```python
import functools

import jax
import jax.numpy as jnp
from jax import lax
from jax.experimental import pallas as pl
from jax.experimental.pallas import tpu as pltpu
from jax.sharding import PartitionSpec as P

W = 30
D = 4
B = 64
SEC_DEV = 8
CLASSES = 5
ITERS = 2


EPSILON = 1e-06
HIGHEST_PRECISION = lax.Precision.HIGHEST


def passed_along(block, axis, distance):
    devices = range(lax.axis_size(axis))
    route = [(i - distance, i) for i in devices if i - distance in devices]
    return lax.ppermute(block, axis, route)


def live_masks(left_sizes, right_sizes, offset):
    row_limit = lax.dynamic_slice_in_dim(left_sizes, offset, SEC_DEV, 0)
    column_limit = lax.dynamic_slice_in_dim(right_sizes, offset, SEC_DEV, 0)
    row_live = jnp.arange(B, dtype=jnp.int32)[None, :] < row_limit[:, None]
    column_live = jnp.arange(B, dtype=jnp.int32)[None, None, :] < column_limit[:, :, None]
    joined_live = row_live[:, :, None, None] & column_live[:, None, :, :]
    return joined_live.astype(jnp.float32).reshape(SEC_DEV, B, D * B)


def step_at(place, group_total):
    return group_total // 2 + (1 - 2 * (place % 2)) * ((place + 1) // 2)


def send_order(group_total):
    return [step_at(place, group_total) for place in range(group_total - 1)]


def pair_tables(target_list, group, group_total):
    steps = send_order(group_total)
    place_of = [group_total - 1] * group_total
    for place, step in enumerate(steps):
        place_of[step] = place
    place_of = jnp.array(place_of, dtype=jnp.int32)
    step_list = (target_list // SEC_DEV - group + group_total) % group_total
    one_hot = step_list[:, None] == jnp.arange(group_total, dtype=jnp.int32)[None, :]
    place_list = jnp.sum(jnp.where(one_hot, place_of[None, :], 0), axis=1)
    order = jnp.arange(SEC_DEV * CLASSES, dtype=jnp.int32)
    sort_key = place_list * (SEC_DEV * CLASSES) + order
    position = jnp.sum((sort_key[None, :] < sort_key[:, None]).astype(jnp.int32), axis=1)
    place_start = jnp.sum(
        (place_list[:, None] < jnp.arange(group_total, dtype=jnp.int32)[None, :]).astype(jnp.int32), axis=0
    )
    own_start = jnp.sum((place_list[None, :] < place_list[:, None]).astype(jnp.int32), axis=1)
    return target_list, place_list, position, place_start, position - own_start


def routing_tables(sector_shift, my_group, group_total, capacity):
    pairs = SEC_DEV * CLASSES
    groups = jnp.arange(group_total, dtype=jnp.int32)
    target_lists = sector_shift.reshape(CLASSES, group_total, SEC_DEV).transpose(1, 2, 0)
    targets, places, positions, starts, ranks = jax.vmap(
        lambda target_list, group: pair_tables(target_list, group, group_total)
    )(target_lists.reshape(group_total, pairs), groups)
    mine = groups == my_group
    my_position = jnp.sum(jnp.where(mine[:, None], positions, 0), axis=0)
    my_start = jnp.sum(jnp.where(mine[:, None], starts, 0), axis=0)
    index = jnp.arange(pairs, dtype=jnp.int32)
    sorted_pair = jnp.sum(jnp.where(my_position[None, :] == index[:, None], index[None, :], 0), axis=1)
    slot_source = (
        my_start[: group_total - 1, None] + jnp.arange(capacity, dtype=jnp.int32)[None, :]
    ).reshape(-1)
    slot_source = jnp.minimum(slot_source, pairs - 1)
    local = targets - my_group * SEC_DEV
    slots = (group_total - 1) * capacity
    value = jnp.where(mine[:, None], slots + positions, places * capacity + ranks)
    wanted = jnp.arange(SEC_DEV, dtype=jnp.int32)
    class_of = index % CLASSES
    hit = (local[None, None, :, :] == wanted[:, None, None, None]) & (
        class_of[None, None, None, :] == jnp.arange(CLASSES, dtype=jnp.int32)[None, :, None, None]
    )
    source = jnp.sum(jnp.where(hit, value[None, None], 0), axis=(2, 3)).reshape(pairs)
    from_self = (source >= slots).astype(jnp.int32)
    arrived_slot = jnp.where(from_self == 1, 0, source)
    own_position = jnp.where(from_self == 1, source - slots, 0)
    return sorted_pair, slot_source, from_self, arrived_slot, own_position


def gate_kernel(mix_ref, right_ref, *refs):
    gate_ref, turned, low, spread = refs[-4:]
    sites, channel_sites, depth = mix_ref.shape
    classes = gate_ref.shape[0]
    bond = right_ref.shape[1]
    halves = bond // 2
    channels = right_ref.shape[2] // bond
    per_class = channel_sites // classes
    low_lanes = lax.broadcasted_iota(jnp.int32, (halves, 128), 1) < 64
    for channel in range(channels, depth):
        turned[pl.ds(channel, halves, stride=depth), :] = jnp.zeros((halves, 128), jnp.float32)
    for pair in range(channels // 2):
        slab = right_ref[0, :, pair * 128 : (pair + 1) * 128].astype(jnp.float32)
        one, two = slab[:halves], slab[halves:]
        turned[pl.ds(2 * pair, halves, stride=depth), :] = jnp.where(
            low_lanes, one, pltpu.roll(two, 64, 1)
        )
        turned[pl.ds(2 * pair + 1, halves, stride=depth), :] = jnp.where(
            low_lanes, pltpu.roll(one, 64, 1), two
        )
    for half in range(halves):
        low[:, half * 128 : (half + 1) * 128] = turned[half * depth : (half + 1) * depth, :].astype(
            jnp.bfloat16
        )
    for site in range(sites):
        for half in range(0, halves, 2):
            mixed = jnp.dot(
                mix_ref[site], low[:, half * 128 : (half + 2) * 128], preferred_element_type=jnp.float32
            )
            spread[site % 2, half * channel_sites : (half + 1) * channel_sites, :] = mixed[:, :128]
            spread[site % 2, (half + 1) * channel_sites : (half + 2) * channel_sites, :] = mixed[:, 128:]

        def one_class(charge, carry):
            for pair in range(per_class // 2):
                first = charge * per_class + 2 * pair
                one = spread[site % 2, pl.ds(first, halves, stride=channel_sites), :]
                two = spread[site % 2, pl.ds(first + 1, halves, stride=channel_sites), :]
                upper = jnp.where(low_lanes, one, pltpu.roll(two, 64, 1))
                lower = jnp.where(low_lanes, pltpu.roll(one, 64, 1), two)
                lanes = slice(pair * 128, (pair + 1) * 128)
                gate_ref[charge, site * bond : site * bond + halves, lanes] = upper.astype(jnp.bfloat16)
                gate_ref[charge, site * bond + halves : (site + 1) * bond, lanes] = lower.astype(
                    jnp.bfloat16
                )
            return carry

        lax.fori_loop(0, classes, one_class, 0)


def environment_kernel(shift_ref, mix_ref, left_ref, site_ref, every_ref, out_ref, spread, turned):
    classes, bond, per_columns = out_ref.shape
    per_class = per_columns // bond
    mixed_rows = mix_ref.shape[0]
    sites = every_ref.shape[2] // bond
    channels = classes * per_class
    halves = bond // 2
    sector = pl.program_id(0)
    sectors = pl.num_programs(0)
    low_lanes = lax.broadcasted_iota(jnp.int32, (halves, 128), 1) < 64
    for charge in range(classes):
        shifted = every_ref[shift_ref[charge * sectors + sector]]
        joined = lax.dot_general(
            shifted,
            left_ref[0, :, charge * per_columns : (charge + 1) * per_columns],
            (((0,), (0,)), ((), ())),
            preferred_element_type=jnp.float32,
        )
        for site in range(sites):
            for pair in range(per_class // 2):
                lanes = slice(pair * 128, (pair + 1) * 128)
                one = joined[site * bond : site * bond + halves, lanes]
                two = joined[site * bond + halves : (site + 1) * bond, lanes]
                row = (charge * per_class + 2 * pair) * sites + site
                spread[pl.ds(row, halves, stride=mixed_rows), :] = jnp.where(
                    low_lanes, one, pltpu.roll(two, 64, 1)
                )
                spread[pl.ds(row + sites, halves, stride=mixed_rows), :] = jnp.where(
                    low_lanes, pltpu.roll(one, 64, 1), two
                )

    def mix_two(half, carry):
        base = pl.multiple_of(half * 2 * mixed_rows, 8)
        after = pl.multiple_of(base + mixed_rows, 8)
        both = jnp.concatenate(
            [spread[pl.ds(base, mixed_rows), :], spread[pl.ds(after, mixed_rows), :]], axis=1
        ).astype(jnp.bfloat16)
        mixed = jnp.dot(mix_ref[...], both, preferred_element_type=jnp.float32)
        spread[pl.ds(base, mixed_rows), :] = mixed[:, :128]
        spread[pl.ds(after, mixed_rows), :] = mixed[:, 128:]
        return carry

    lax.fori_loop(0, halves // 2, mix_two, 0, unroll=4)
    for channel in range(channels):
        for pair in range(sites // 2):
            row = channel * sites + 2 * pair
            one = spread[pl.ds(row, halves, stride=mixed_rows), :]
            two = spread[pl.ds(row + 1, halves, stride=mixed_rows), :]
            lanes = slice(pair * 128, (pair + 1) * 128)
            turned[channel * bond : channel * bond + halves, lanes] = jnp.where(
                low_lanes, one, pltpu.roll(two, 64, 1)
            ).astype(jnp.bfloat16)
            turned[channel * bond + halves : (channel + 1) * bond, lanes] = jnp.where(
                low_lanes, pltpu.roll(one, 64, 1), two
            ).astype(jnp.bfloat16)
    for charge in range(classes):
        rows = slice(charge * per_columns, (charge + 1) * per_columns)
        built = jnp.dot(turned[rows, :], site_ref[0], preferred_element_type=jnp.float32)
        for pair in range(per_class // 2):
            one = built[2 * pair * bond : (2 * pair + 1) * bond]
            two = built[(2 * pair + 1) * bond : (2 * pair + 2) * bond]
            out_ref[charge, :, pair * 128 : (pair + 1) * 128] = jnp.concatenate(
                [one, two], axis=1
            ).astype(jnp.bfloat16)


def build_environment(environment, site_blocks, channel_mix, sector_shift, offset, gate):
    every_site = lax.all_gather(site_blocks, "sec", axis=0, tiled=True)
    every_site, gate = lax.optimization_barrier((every_site, gate))
    sectors = environment.shape[0]
    targets = lax.dynamic_slice_in_dim(sector_shift, offset, sectors, 1).reshape(-1)
    mix = channel_mix.transpose(2, 3, 0, 1).reshape(W * D, W * D)
    own = site_blocks.reshape(sectors, B, D, B).transpose(0, 2, 1, 3).reshape(sectors, D * B, B)
    per_columns = W // CLASSES * B
    fresh = pl.pallas_call(
        environment_kernel,
        grid=(sectors,),
        in_specs=[
            pl.BlockSpec(memory_space=pltpu.SMEM),
            pl.BlockSpec((W * D, W * D), lambda sector: (0, 0)),
            pl.BlockSpec((1, B, W * B), lambda sector: (sector, 0, 0)),
            pl.BlockSpec((1, D * B, B), lambda sector: (sector, 0, 0)),
            pl.BlockSpec(every_site.shape, lambda sector: (0, 0, 0)),
        ],
        out_specs=pl.BlockSpec((CLASSES, B, per_columns), lambda sector: (sector, 0, 0)),
        out_shape=jax.ShapeDtypeStruct((sectors * CLASSES, B, per_columns), jnp.bfloat16),
        scratch_shapes=[
            pltpu.VMEM((B // 2 * W * D, 2 * B), jnp.float32),
            pltpu.VMEM((W * B, D * B), jnp.bfloat16),
        ],
        compiler_params=pltpu.CompilerParams(vmem_limit_bytes=32 * 1024 * 1024),
        cost_estimate=pl.CostEstimate(
            flops=8 * sectors * W * D * W * D * B * B, bytes_accessed=6000000, transcendentals=0
        ),
    )(targets, mix, environment, own, every_site)
    return fresh, gate


def build_gate(right_used, channel_mix, begin, end, gate):
    sectors = right_used.shape[0]
    halves = B // 2
    depth = (W + 15) // 16 * 16
    mix = channel_mix.transpose(3, 0, 1, 2).reshape(D, W * D, W)
    mix = jnp.pad(mix, ((0, 0), (0, 0), (0, depth - W)))
    shape = (sectors * CLASSES, D * B, W // CLASSES * D * B)
    earlier = () if gate is None else (gate,)
    return pl.pallas_call(
        gate_kernel,
        grid=(end - begin,),
        in_specs=[
            pl.BlockSpec(mix.shape, lambda sector: (0, 0, 0)),
            pl.BlockSpec((1, B, W * B), lambda sector: (sector + begin, 0, 0)),
        ]
        + [pl.BlockSpec(memory_space=pl.ANY)] * len(earlier),
        out_specs=pl.BlockSpec((CLASSES,) + shape[1:], lambda sector: (sector + begin, 0, 0)),
        out_shape=jax.ShapeDtypeStruct(shape, jnp.bfloat16),
        input_output_aliases={2: 0} if earlier else {},
        scratch_shapes=[
            pltpu.VMEM((halves * depth, 2 * B), jnp.float32),
            pltpu.VMEM((depth, B * B), jnp.bfloat16),
            pltpu.VMEM((2, halves * W * D, 2 * B), jnp.float32),
        ],
        compiler_params=pltpu.CompilerParams(vmem_limit_bytes=32 * 1024 * 1024),
        cost_estimate=pl.CostEstimate(
            flops=16 * (end - begin) * D * W * D * W * B * B,
            bytes_accessed=8000000 * (end - begin),
            transcendentals=0,
        ),
    )(mix, right_used, *earlier)


def davidson_kernel(
    n,
    capacity,
    total_entries,
    pair_ref,
    slot_ref,
    self_ref,
    arrived_ref,
    own_ref,
    mask_ref,
    start_ref,
    precondition_ref,
    left_ref,
    gate_ref,
    state_ref,
    energy_ref,
    current,
    applied,
    direction,
    product,
    low,
    stacked,
    partial,
    outgoing,
    incoming,
    row_send,
    row_all,
    send_sem,
    recv_sem,
    row_send_sem,
    row_recv_sem,
):
    pairs = left_ref.shape[0]
    sectors, rows, columns = current.shape
    classes = pairs // sectors
    channels = left_ref.shape[2] // rows
    steps = send_order(n)
    me = lax.axis_index("sec")

    barrier = pltpu.get_barrier_semaphore()
    for step in steps:
        pl.semaphore_signal(
            barrier,
            inc=1,
            device_id={"sec": lax.rem(me + step, n)},
            device_id_type=pl.DeviceIdType.MESH,
        )
    pl.semaphore_wait(barrier, n - 1)

    def fold(values):
        eight = jnp.sum(values.reshape(rows // 8, 8, columns), axis=0)
        return eight[:, : columns // 2] + eight[:, columns // 2 :]

    def all_sums(turn, count, products):
        zero = jnp.zeros((8, columns // 2), jnp.float32)

        def body(sector, sums):
            return tuple(total + fold(term) for total, term in zip(sums, products(sector)))

        sums = lax.fori_loop(0, sectors, body, (zero,) * count)
        for entry in range(8):
            if entry < count:
                row_send[turn, entry : entry + 1, :] = jnp.sum(sums[entry], axis=0, keepdims=True)
            else:
                row_send[turn, entry : entry + 1, :] = zero[0:1]
        copies = []
        for place, step in enumerate(steps):
            copies.append(
                pltpu.make_async_remote_copy(
                    src_ref=row_send.at[turn],
                    dst_ref=row_all.at[turn, me],
                    send_sem=row_send_sem.at[turn, place],
                    recv_sem=row_recv_sem.at[turn, place],
                    device_id={"sec": lax.rem(me + step, n)},
                    device_id_type=pl.DeviceIdType.MESH,
                )
            )
            copies[-1].start()
        row_all[turn, me] = row_send[turn]
        for copy in copies:
            copy.wait()
        whole = row_all[turn, 0]
        for group in range(1, n):
            whole = whole + row_all[turn, group]
        whole = jnp.sum(whole, axis=1, keepdims=True) / total_entries
        return [whole[entry : entry + 1, :] for entry in range(count)]

    def operator(turn, result):
        def one_pair(position, slot):
            pair = pair_ref[position]
            sector = pair_ref[pairs + position]
            mixed = jnp.dot(low[sector], gate_ref[pair], preferred_element_type=jnp.float32)
            for channel in range(channels):
                stacked[slot, channel * rows : (channel + 1) * rows, :] = mixed[
                    :, channel * columns : (channel + 1) * columns
                ].astype(jnp.bfloat16)
            partial[position] = jnp.dot(
                left_ref[pair], stacked[slot], preferred_element_type=jnp.float32
            )

        def copy_at(place):
            return pltpu.make_async_remote_copy(
                src_ref=outgoing.at[turn, place],
                dst_ref=incoming.at[turn, place],
                send_sem=send_sem.at[turn, place],
                recv_sem=recv_sem.at[turn, place],
                device_id={"sec": lax.rem(me + step_at(place, n), n)},
                device_id_type=pl.DeviceIdType.MESH,
            )

        def send(place):
            for rank in range(capacity):
                outgoing[turn, place, rank] = partial[slot_ref[place * capacity + rank]].astype(
                    jnp.bfloat16
                )
            copy_at(place).start()

        def one_place(place, carry):
            for rank in range(capacity):
                one_pair(place * capacity + rank, rank)
            send(place)
            return carry

        whole_places = min(pairs // capacity, n - 1)
        lax.fori_loop(0, whole_places, one_place, 0)
        for position in range(whole_places * capacity, pairs):
            one_pair(position, position % capacity)
        for place in range(whole_places, n - 1):
            send(place)

        def wait_for(place, carry):
            copy_at(place).wait()
            return carry

        lax.fori_loop(0, n - 1, wait_for, 0)
        landed = incoming.at[turn]

        def gather(sector, carry):
            total = jnp.zeros((rows, columns), jnp.float32)
            for charge in range(classes):
                entry = sector * classes + charge
                slot = arrived_ref[entry]
                came = landed[arrived_ref[pairs + entry], slot].astype(jnp.float32)
                own = partial[own_ref[entry]]
                own_part = jnp.broadcast_to(self_ref[entry], (rows, columns)) == 1
                total = total + jnp.where(own_part, own, came)
            result[sector] = mask_ref[sector] * total
            return carry

        lax.fori_loop(0, sectors, gather, 0)

    def first(sector, carry):
        current[sector] = mask_ref[sector] * start_ref[sector]
        return carry

    lax.fori_loop(0, sectors, first, 0)
    (start_square,) = all_sums(0, 1, lambda s: (current[s] * current[s],))
    start_scale = 1.0 / jnp.sqrt(start_square + EPSILON)

    def normalise(sector, carry):
        value = current[sector] * start_scale
        current[sector] = value
        low[sector] = value.astype(jnp.bfloat16)
        return carry

    lax.fori_loop(0, sectors, normalise, 0)
    operator(0, applied)
    energy = None
    for iteration in range(ITERS):

        def shaped(sector):
            one, two = current[sector], applied[sector]
            weight = precondition_ref[sector]
            weighted_one, weighted_two = weight * one, weight * two
            return (
                one * two,
                one * one,
                one * weighted_two,
                one * weighted_one,
                weighted_two * weighted_two,
                weighted_two * weighted_one,
                weighted_one * weighted_one,
            )

        sums = all_sums(1 + 2 * iteration, 7, shaped)
        rho = sums[0]
        correlation = sums[2] - rho * sums[3]
        square = sums[4] - 2.0 * rho * sums[5] + rho * rho * sums[6]
        square = square - 2.0 * correlation * correlation + correlation * correlation * sums[1]
        scale = 1.0 / jnp.sqrt(jnp.maximum(square, 0.0) + EPSILON)

        def correct(sector, carry):
            one = current[sector]
            value = precondition_ref[sector] * (applied[sector] - rho * one)
            value = (value - correlation * one) * scale
            direction[sector] = value
            low[sector] = value.astype(jnp.bfloat16)
            return carry

        lax.fori_loop(0, sectors, correct, 0)
        operator(1 + iteration, product)
        sums = all_sums(
            2 + 2 * iteration,
            3,
            lambda s: (current[s] * product[s], direction[s] * applied[s], direction[s] * product[s]),
        )
        cross = 0.5 * (sums[0] + sums[1])
        far = sums[2]
        across, along = -2.0 * cross, far - rho
        largest = jnp.maximum(jnp.abs(across), jnp.abs(along))
        still = largest == 0.0
        safe = jnp.where(still, 1.0, largest)
        across, along = across / safe, jnp.where(still, 1.0, along / safe)
        length = jnp.sqrt(across * across + along * along)
        bigger = jnp.sqrt(0.5 * (length + jnp.abs(along)) / length)
        smaller = 0.5 * jnp.abs(across) / (length * bigger)
        ahead = along >= 0.0
        cosine = jnp.where(ahead, bigger, smaller)
        sine = jnp.where(ahead, smaller, bigger)
        sine = jnp.where(across > 0.0, sine, -sine)
        energy = cosine * cosine * rho + 2.0 * cosine * sine * cross + sine * sine * far
        last = iteration == ITERS - 1

        def rotate(sector, carry):
            value = cosine * current[sector] + sine * direction[sector]
            if last:
                state_ref[sector] = value
            else:
                current[sector] = value
                applied[sector] = cosine * applied[sector] + sine * product[sector]
            return carry

        lax.fori_loop(0, sectors, rotate, 0)
    energy_ref[...] = jnp.broadcast_to(energy, energy_ref.shape)


def davidson(tables, live_mask, start, precondition, left_pairs, gate, group_total, capacity):
    pairs = left_pairs.shape[0]
    sectors, rows, columns = start.shape
    sorted_pair, slot_source, from_self, arrived_slot, own_position = tables
    sorted_pair = jnp.concatenate([sorted_pair, sorted_pair // CLASSES])
    arrived_slot = jnp.concatenate([arrived_slot % capacity, arrived_slot // capacity])
    turns = ITERS + 1
    rounds = 2 * ITERS + 1
    others = group_total - 1
    smem = pl.BlockSpec(memory_space=pltpu.SMEM)
    vmem = pl.BlockSpec(memory_space=pltpu.VMEM)
    vector = pltpu.VMEM((sectors, rows, columns), jnp.float32)
    kernel = functools.partial(
        davidson_kernel, group_total, capacity, float(group_total * sectors * rows * columns)
    )
    return pl.pallas_call(
        kernel,
        out_shape=(
            jax.ShapeDtypeStruct(start.shape, jnp.float32),
            jax.ShapeDtypeStruct((8, 128), jnp.float32),
        ),
        in_specs=[smem] * 5 + [vmem] * 5,
        out_specs=(vmem, vmem),
        scratch_shapes=[
            vector,
            vector,
            vector,
            vector,
            pltpu.VMEM((sectors, rows, columns), jnp.bfloat16),
            pltpu.VMEM((capacity, left_pairs.shape[2], columns), jnp.bfloat16),
            pltpu.VMEM((pairs, rows, columns), jnp.float32),
            pltpu.VMEM((turns, others, capacity, rows, columns), jnp.bfloat16),
            pltpu.VMEM((turns, others, capacity, rows, columns), jnp.bfloat16),
            pltpu.VMEM((rounds, 8, columns // 2), jnp.float32),
            pltpu.VMEM((rounds, group_total, 8, columns // 2), jnp.float32),
            pltpu.SemaphoreType.DMA((turns, others)),
            pltpu.SemaphoreType.DMA((turns, others)),
            pltpu.SemaphoreType.DMA((rounds, others)),
            pltpu.SemaphoreType.DMA((rounds, others)),
        ],
        compiler_params=pltpu.CompilerParams(
            collective_id=0, has_side_effects=True, vmem_limit_bytes=58 * 1024 * 1024
        ),
    )(
        sorted_pair,
        slot_source,
        from_self,
        arrived_slot,
        own_position,
        live_mask,
        start,
        precondition,
        left_pairs,
        gate,
    )


def on_device(
    left_environment,
    right_environment,
    site_previous,
    state_start,
    preconditioner,
    channel_tensor,
    channel_mask,
    sector_shift,
    left_sizes,
    right_sizes,
):
    group_total = lax.axis_size("sec")
    my_group = lax.axis_index("sec")
    offset = my_group * SEC_DEV
    capacity = (CLASSES * SEC_DEV + group_total - 1) // group_total
    channel_mix = channel_tensor * channel_mask.astype(jnp.bfloat16)[:, None, :, None]
    live_mask = live_masks(left_sizes, right_sizes, offset)
    own_left = left_environment[0]
    position = lax.axis_index("seg")
    came_right = passed_along(right_environment[0], "seg", -1)
    right_used = jnp.where(position == lax.axis_size("seg") - 1, right_environment[0], came_right)
    gate = build_gate(right_used, channel_mix, 0, SEC_DEV // 2, None)
    fresh, gate = build_environment(
        own_left, site_previous[0], channel_mix, sector_shift, offset, gate
    )
    handed = passed_along(fresh, "seg", 1)
    own_pairs = (
        own_left.reshape(SEC_DEV, B, CLASSES, W // CLASSES * B)
        .transpose(0, 2, 1, 3)
        .reshape(SEC_DEV * CLASSES, B, W // CLASSES * B)
    )
    left_pairs = jnp.where(position == 0, own_pairs, handed)
    gate = build_gate(right_used, channel_mix, SEC_DEV // 2, SEC_DEV, gate)
    tables = routing_tables(sector_shift, my_group, group_total, capacity)
    state, energy = davidson(
        tables, live_mask, state_start[0], preconditioner[0], left_pairs, gate, group_total, capacity
    )
    return (state[None], energy[0, 0:1])


def solution(mesh):
    in_specs = (
        P("seg", "sec", None, None),
        P("seg", "sec", None, None),
        P("seg", "sec", None, None),
        P("seg", "sec", None, None),
        P("seg", "sec", None, None),
        P(),
        P(),
        P(),
        P(),
        P(),
    )
    out_specs = (P("seg", "sec", None, None), P("seg"))
    return jax.shard_map(
        on_device, mesh=mesh, in_specs=in_specs, out_specs=out_specs, check_vma=False
    )
```

```python
import functools

import jax
import jax.numpy as jnp
from jax import lax
from jax.experimental import pallas as pl
from jax.experimental.pallas import tpu as pltpu
from jax.sharding import PartitionSpec as P

W = 30
D = 4
B = 64
SEC_DEV = 8
CLASSES = 5
ITERS = 2


EPSILON = 1e-06
HIGHEST_PRECISION = lax.Precision.HIGHEST


def passed_along(block, axis, distance):
    devices = range(lax.axis_size(axis))
    route = [(i - distance, i) for i in devices if i - distance in devices]
    return lax.ppermute(block, axis, route)


def live_masks(left_sizes, right_sizes, offset):
    row_limit = lax.dynamic_slice_in_dim(left_sizes, offset, SEC_DEV, 0)
    column_limit = lax.dynamic_slice_in_dim(right_sizes, offset, SEC_DEV, 0)
    row_live = jnp.arange(B, dtype=jnp.int32)[None, :] < row_limit[:, None]
    column_live = jnp.arange(B, dtype=jnp.int32)[None, None, :] < column_limit[:, :, None]
    joined_live = row_live[:, :, None, None] & column_live[:, None, :, :]
    return joined_live.astype(jnp.float32).reshape(SEC_DEV, B, D * B)


def step_at(place, group_total):
    return group_total // 2 + (1 - 2 * (place % 2)) * ((place + 1) // 2)


def send_order(group_total):
    return [step_at(place, group_total) for place in range(group_total - 1)]


def pair_tables(target_list, group, group_total):
    steps = send_order(group_total)
    place_of = [group_total - 1] * group_total
    for place, step in enumerate(steps):
        place_of[step] = place
    place_of = jnp.array(place_of, dtype=jnp.int32)
    step_list = (target_list // SEC_DEV - group + group_total) % group_total
    one_hot = step_list[:, None] == jnp.arange(group_total, dtype=jnp.int32)[None, :]
    place_list = jnp.sum(jnp.where(one_hot, place_of[None, :], 0), axis=1)
    order = jnp.arange(SEC_DEV * CLASSES, dtype=jnp.int32)
    sort_key = place_list * (SEC_DEV * CLASSES) + order
    position = jnp.sum((sort_key[None, :] < sort_key[:, None]).astype(jnp.int32), axis=1)
    place_start = jnp.sum(
        (place_list[:, None] < jnp.arange(group_total, dtype=jnp.int32)[None, :]).astype(jnp.int32), axis=0
    )
    own_start = jnp.sum((place_list[None, :] < place_list[:, None]).astype(jnp.int32), axis=1)
    return target_list, place_list, position, place_start, position - own_start


def routing_tables(sector_shift, my_group, group_total, capacity):
    pairs = SEC_DEV * CLASSES
    groups = jnp.arange(group_total, dtype=jnp.int32)
    target_lists = sector_shift.reshape(CLASSES, group_total, SEC_DEV).transpose(1, 2, 0)
    targets, places, positions, starts, ranks = jax.vmap(
        lambda target_list, group: pair_tables(target_list, group, group_total)
    )(target_lists.reshape(group_total, pairs), groups)
    mine = groups == my_group
    my_position = jnp.sum(jnp.where(mine[:, None], positions, 0), axis=0)
    my_start = jnp.sum(jnp.where(mine[:, None], starts, 0), axis=0)
    index = jnp.arange(pairs, dtype=jnp.int32)
    sorted_pair = jnp.sum(jnp.where(my_position[None, :] == index[:, None], index[None, :], 0), axis=1)
    slot_source = (
        my_start[: group_total - 1, None] + jnp.arange(capacity, dtype=jnp.int32)[None, :]
    ).reshape(-1)
    slot_source = jnp.minimum(slot_source, pairs - 1)
    local = targets - my_group * SEC_DEV
    slots = (group_total - 1) * capacity
    value = jnp.where(mine[:, None], slots + positions, places * capacity + ranks)
    wanted = jnp.arange(SEC_DEV, dtype=jnp.int32)
    class_of = index % CLASSES
    hit = (local[None, None, :, :] == wanted[:, None, None, None]) & (
        class_of[None, None, None, :] == jnp.arange(CLASSES, dtype=jnp.int32)[None, :, None, None]
    )
    source = jnp.sum(jnp.where(hit, value[None, None], 0), axis=(2, 3)).reshape(pairs)
    from_self = (source >= slots).astype(jnp.int32)
    arrived_slot = jnp.where(from_self == 1, 0, source)
    own_position = jnp.where(from_self == 1, source - slots, 0)
    return sorted_pair, slot_source, from_self, arrived_slot, own_position


def gate_kernel(mix_ref, right_ref, *refs):
    gate_ref, turned, low, spread = refs[-4:]
    depth = mix_ref.shape[1]
    classes = gate_ref.shape[0]
    bond = right_ref.shape[1]
    sites = gate_ref.shape[1] // bond
    channel_sites = mix_ref.shape[0] // sites
    halves = bond // 2
    channels = right_ref.shape[2] // bond
    per_class = channel_sites // classes
    low_lanes = lax.broadcasted_iota(jnp.int32, (halves, 128), 1) < 64
    for channel in range(channels, depth):
        turned[pl.ds(channel, halves, stride=depth), :] = jnp.zeros((halves, 128), jnp.float32)
    for pair in range(channels // 2):
        slab = right_ref[0, :, pair * 128 : (pair + 1) * 128].astype(jnp.float32)
        one, two = slab[:halves], slab[halves:]
        turned[pl.ds(2 * pair, halves, stride=depth), :] = jnp.where(
            low_lanes, one, pltpu.roll(two, 64, 1)
        )
        turned[pl.ds(2 * pair + 1, halves, stride=depth), :] = jnp.where(
            low_lanes, pltpu.roll(one, 64, 1), two
        )
    for half in range(halves):
        low[:, half * 128 : (half + 1) * 128] = turned[half * depth : (half + 1) * depth, :].astype(
            jnp.bfloat16
        )
    for half in range(0, halves, 2):
        mixed = jnp.dot(
            mix_ref[...], low[:, half * 128 : (half + 2) * 128], preferred_element_type=jnp.float32
        )
        for site in range(sites):
            rows = slice(site * channel_sites, (site + 1) * channel_sites)
            spread[site, half * channel_sites : (half + 1) * channel_sites, :] = mixed[rows, :128]
            spread[site, (half + 1) * channel_sites : (half + 2) * channel_sites, :] = mixed[rows, 128:]

    def one_class(charge, carry):
        for site in range(sites):
            for pair in range(per_class // 2):
                first = charge * per_class + 2 * pair
                one = spread[site, pl.ds(first, halves, stride=channel_sites), :]
                two = spread[site, pl.ds(first + 1, halves, stride=channel_sites), :]
                upper = jnp.where(low_lanes, one, pltpu.roll(two, 64, 1))
                lower = jnp.where(low_lanes, pltpu.roll(one, 64, 1), two)
                lanes = slice(pair * 128, (pair + 1) * 128)
                gate_ref[charge, site * bond : site * bond + halves, lanes] = upper.astype(jnp.bfloat16)
                gate_ref[charge, site * bond + halves : (site + 1) * bond, lanes] = lower.astype(
                    jnp.bfloat16
                )
        return carry

    lax.fori_loop(0, classes, one_class, 0)


def environment_kernel(shift_ref, mix_ref, left_ref, site_ref, every_ref, out_ref, own_ref, spread, turned):
    classes, bond, per_columns = out_ref.shape
    per_class = per_columns // bond
    mixed_rows = mix_ref.shape[0]
    sites = every_ref.shape[2] // bond
    channels = classes * per_class
    halves = bond // 2
    sector = pl.program_id(0)
    sectors = pl.num_programs(0)
    low_lanes = lax.broadcasted_iota(jnp.int32, (halves, 128), 1) < 64
    for charge in range(classes):
        own_ref[charge] = left_ref[0, :, charge * per_columns : (charge + 1) * per_columns]
        shifted = every_ref[shift_ref[charge * sectors + sector]]
        joined = lax.dot_general(
            shifted,
            left_ref[0, :, charge * per_columns : (charge + 1) * per_columns],
            (((0,), (0,)), ((), ())),
            preferred_element_type=jnp.float32,
        )
        for site in range(sites):
            for pair in range(per_class // 2):
                lanes = slice(pair * 128, (pair + 1) * 128)
                one = joined[site * bond : site * bond + halves, lanes]
                two = joined[site * bond + halves : (site + 1) * bond, lanes]
                row = (charge * per_class + 2 * pair) * sites + site
                spread[pl.ds(row, halves, stride=mixed_rows), :] = jnp.where(
                    low_lanes, one, pltpu.roll(two, 64, 1)
                )
                spread[pl.ds(row + sites, halves, stride=mixed_rows), :] = jnp.where(
                    low_lanes, pltpu.roll(one, 64, 1), two
                )

    def mix_two(half, carry):
        base = pl.multiple_of(half * 2 * mixed_rows, 8)
        after = pl.multiple_of(base + mixed_rows, 8)
        both = jnp.concatenate(
            [spread[pl.ds(base, mixed_rows), :], spread[pl.ds(after, mixed_rows), :]], axis=1
        ).astype(jnp.bfloat16)
        mixed = jnp.dot(mix_ref[...], both, preferred_element_type=jnp.float32)
        spread[pl.ds(base, mixed_rows), :] = mixed[:, :128]
        spread[pl.ds(after, mixed_rows), :] = mixed[:, 128:]
        return carry

    lax.fori_loop(0, halves // 2, mix_two, 0, unroll=4)
    for channel in range(channels):
        for pair in range(sites // 2):
            row = channel * sites + 2 * pair
            one = spread[pl.ds(row, halves, stride=mixed_rows), :]
            two = spread[pl.ds(row + 1, halves, stride=mixed_rows), :]
            lanes = slice(pair * 128, (pair + 1) * 128)
            turned[channel * bond : channel * bond + halves, lanes] = jnp.where(
                low_lanes, one, pltpu.roll(two, 64, 1)
            ).astype(jnp.bfloat16)
            turned[channel * bond + halves : (channel + 1) * bond, lanes] = jnp.where(
                low_lanes, pltpu.roll(one, 64, 1), two
            ).astype(jnp.bfloat16)
    for charge in range(classes):
        rows = slice(charge * per_columns, (charge + 1) * per_columns)
        built = jnp.dot(turned[rows, :], site_ref[0], preferred_element_type=jnp.float32)
        for pair in range(per_class // 2):
            one = built[2 * pair * bond : (2 * pair + 1) * bond]
            two = built[(2 * pair + 1) * bond : (2 * pair + 2) * bond]
            out_ref[charge, :, pair * 128 : (pair + 1) * 128] = jnp.concatenate(
                [one, two], axis=1
            ).astype(jnp.bfloat16)


def build_environment(environment, site_blocks, channel_mix, sector_shift, offset, gate):
    every_site = lax.all_gather(site_blocks, "sec", axis=0, tiled=True)
    every_site, gate = lax.optimization_barrier((every_site, gate))
    sectors = environment.shape[0]
    targets = lax.dynamic_slice_in_dim(sector_shift, offset, sectors, 1).reshape(-1)
    mix = channel_mix.transpose(2, 3, 0, 1).reshape(W * D, W * D)
    own = site_blocks.reshape(sectors, B, D, B).transpose(0, 2, 1, 3).reshape(sectors, D * B, B)
    per_columns = W // CLASSES * B
    pairs = pl.BlockSpec((CLASSES, B, per_columns), lambda sector: (sector, 0, 0))
    shape = jax.ShapeDtypeStruct((sectors * CLASSES, B, per_columns), jnp.bfloat16)
    fresh, own_pairs = pl.pallas_call(
        environment_kernel,
        grid=(sectors,),
        in_specs=[
            pl.BlockSpec(memory_space=pltpu.SMEM),
            pl.BlockSpec((W * D, W * D), lambda sector: (0, 0)),
            pl.BlockSpec((1, B, W * B), lambda sector: (sector, 0, 0)),
            pl.BlockSpec((1, D * B, B), lambda sector: (sector, 0, 0)),
            pl.BlockSpec(every_site.shape, lambda sector: (0, 0, 0)),
        ],
        out_specs=(pairs, pairs),
        out_shape=(shape, shape),
        scratch_shapes=[
            pltpu.VMEM((B // 2 * W * D, 2 * B), jnp.float32),
            pltpu.VMEM((W * B, D * B), jnp.bfloat16),
        ],
        compiler_params=pltpu.CompilerParams(vmem_limit_bytes=32 * 1024 * 1024),
        cost_estimate=pl.CostEstimate(
            flops=8 * sectors * W * D * W * D * B * B, bytes_accessed=6000000, transcendentals=0
        ),
    )(targets, mix, environment, own, every_site)
    return fresh, own_pairs, gate


def build_gate(right_used, channel_mix, begin, end, gate):
    sectors = right_used.shape[0]
    halves = B // 2
    depth = (W + 15) // 16 * 16
    mix = channel_mix.transpose(3, 0, 1, 2).reshape(D * W * D, W)
    mix = jnp.pad(mix, ((0, 0), (0, depth - W)))
    shape = (sectors * CLASSES, D * B, W // CLASSES * D * B)
    earlier = () if gate is None else (gate,)
    return pl.pallas_call(
        gate_kernel,
        grid=(end - begin,),
        in_specs=[
            pl.BlockSpec(mix.shape, lambda sector: (0, 0)),
            pl.BlockSpec((1, B, W * B), lambda sector: (sector + begin, 0, 0)),
        ]
        + [pl.BlockSpec(memory_space=pl.ANY)] * len(earlier),
        out_specs=pl.BlockSpec((CLASSES,) + shape[1:], lambda sector: (sector + begin, 0, 0)),
        out_shape=jax.ShapeDtypeStruct(shape, jnp.bfloat16),
        input_output_aliases={2: 0} if earlier else {},
        scratch_shapes=[
            pltpu.VMEM((halves * depth, 2 * B), jnp.float32),
            pltpu.VMEM((depth, B * B), jnp.bfloat16),
            pltpu.VMEM((D, halves * W * D, 2 * B), jnp.float32),
        ],
        compiler_params=pltpu.CompilerParams(vmem_limit_bytes=32 * 1024 * 1024),
        cost_estimate=pl.CostEstimate(
            flops=16 * (end - begin) * D * W * D * W * B * B,
            bytes_accessed=8000000 * (end - begin),
            transcendentals=0,
        ),
    )(mix, right_used, *earlier)


def davidson_kernel(
    n,
    capacity,
    total_entries,
    pair_ref,
    slot_ref,
    self_ref,
    arrived_ref,
    own_ref,
    mask_ref,
    start_ref,
    precondition_ref,
    left_ref,
    gate_source,
    state_ref,
    energy_ref,
    current,
    applied,
    direction,
    product,
    low,
    stacked,
    partial,
    outgoing,
    incoming,
    row_send,
    row_all,
    send_sem,
    recv_sem,
    row_send_sem,
    row_recv_sem,
    gate_ref,
    gate_sem,
):
    pairs = left_ref.shape[0]
    sectors, rows, columns = current.shape
    classes = pairs // sectors
    channels = left_ref.shape[2] // rows
    steps = send_order(n)
    me = lax.axis_index("sec")
    gate_copies = []
    for sector in range(sectors):
        part = pl.ds(sector * classes, classes)
        gate_copies.append(
            pltpu.make_async_copy(gate_source.at[part], gate_ref.at[part], gate_sem.at[sector])
        )
        gate_copies[-1].start()

    barrier = pltpu.get_barrier_semaphore()
    for step in steps:
        pl.semaphore_signal(
            barrier,
            inc=1,
            device_id={"sec": lax.rem(me + step, n)},
            device_id_type=pl.DeviceIdType.MESH,
        )
    pl.semaphore_wait(barrier, n - 1)

    def fold(values):
        eight = jnp.sum(values.reshape(rows // 8, 8, columns), axis=0)
        return eight[:, : columns // 2] + eight[:, columns // 2 :]

    def all_sums(turn, count, products):
        zero = jnp.zeros((8, columns // 2), jnp.float32)

        def body(sector, sums):
            return tuple(total + fold(term) for total, term in zip(sums, products(sector)))

        sums = lax.fori_loop(0, sectors, body, (zero,) * count)
        for entry in range(8):
            if entry < count:
                row_send[turn, entry : entry + 1, :] = jnp.sum(sums[entry], axis=0, keepdims=True)
            else:
                row_send[turn, entry : entry + 1, :] = zero[0:1]
        copies = []
        for place, step in enumerate(steps):
            copies.append(
                pltpu.make_async_remote_copy(
                    src_ref=row_send.at[turn],
                    dst_ref=row_all.at[turn, me],
                    send_sem=row_send_sem.at[turn, place],
                    recv_sem=row_recv_sem.at[turn, place],
                    device_id={"sec": lax.rem(me + step, n)},
                    device_id_type=pl.DeviceIdType.MESH,
                )
            )
            copies[-1].start()
        row_all[turn, me] = row_send[turn]
        for copy in copies:
            copy.wait()
        whole = row_all[turn, 0]
        for group in range(1, n):
            whole = whole + row_all[turn, group]
        whole = jnp.sum(whole, axis=1, keepdims=True) / total_entries
        return [whole[entry : entry + 1, :] for entry in range(count)]

    def operator(turn, result):
        def one_pair(position, slot):
            pair = pair_ref[position]
            sector = pair_ref[pairs + position]
            mixed = jnp.dot(low[sector], gate_ref[pair], preferred_element_type=jnp.float32)
            for channel in range(channels):
                stacked[slot, channel * rows : (channel + 1) * rows, :] = mixed[
                    :, channel * columns : (channel + 1) * columns
                ].astype(jnp.bfloat16)
            partial[position] = jnp.dot(
                left_ref[pair], stacked[slot], preferred_element_type=jnp.float32
            )

        def copy_at(place):
            return pltpu.make_async_remote_copy(
                src_ref=outgoing.at[turn, place],
                dst_ref=incoming.at[turn, place],
                send_sem=send_sem.at[turn, place],
                recv_sem=recv_sem.at[turn, place],
                device_id={"sec": lax.rem(me + step_at(place, n), n)},
                device_id_type=pl.DeviceIdType.MESH,
            )

        def send(place):
            for rank in range(capacity):
                outgoing[turn, place, rank] = partial[slot_ref[place * capacity + rank]].astype(
                    jnp.bfloat16
                )
            copy_at(place).start()

        def one_place(place, carry):
            for rank in range(capacity):
                one_pair(place * capacity + rank, rank)
            send(place)
            return carry

        whole_places = min(pairs // capacity, n - 1)
        lax.fori_loop(0, whole_places, one_place, 0)
        for position in range(whole_places * capacity, pairs):
            one_pair(position, position % capacity)
        for place in range(whole_places, n - 1):
            send(place)

        def wait_for(place, carry):
            copy_at(place).wait()
            return carry

        lax.fori_loop(0, n - 1, wait_for, 0)
        landed = incoming.at[turn]

        def gather(sector, carry):
            total = jnp.zeros((rows, columns), jnp.float32)
            for charge in range(classes):
                entry = sector * classes + charge
                slot = arrived_ref[entry]
                came = landed[arrived_ref[pairs + entry], slot].astype(jnp.float32)
                own = partial[own_ref[entry]]
                own_part = jnp.broadcast_to(self_ref[entry], (rows, columns)) == 1
                total = total + jnp.where(own_part, own, came)
            result[sector] = mask_ref[sector] * total
            return carry

        lax.fori_loop(0, sectors, gather, 0)

    def first(sector, carry):
        current[sector] = mask_ref[sector] * start_ref[sector]
        return carry

    lax.fori_loop(0, sectors, first, 0)
    (start_square,) = all_sums(0, 1, lambda s: (current[s] * current[s],))
    start_scale = 1.0 / jnp.sqrt(start_square + EPSILON)

    def normalise(sector, carry):
        value = current[sector] * start_scale
        current[sector] = value
        low[sector] = value.astype(jnp.bfloat16)
        return carry

    lax.fori_loop(0, sectors, normalise, 0)
    for copy in gate_copies:
        copy.wait()
    operator(0, applied)
    energy = None
    for iteration in range(ITERS):

        def shaped(sector):
            one, two = current[sector], applied[sector]
            weight = precondition_ref[sector]
            weighted_one, weighted_two = weight * one, weight * two
            return (
                one * two,
                one * one,
                one * weighted_two,
                one * weighted_one,
                weighted_two * weighted_two,
                weighted_two * weighted_one,
                weighted_one * weighted_one,
            )

        sums = all_sums(1 + 2 * iteration, 7, shaped)
        rho = sums[0]
        correlation = sums[2] - rho * sums[3]
        square = sums[4] - 2.0 * rho * sums[5] + rho * rho * sums[6]
        square = square - 2.0 * correlation * correlation + correlation * correlation * sums[1]
        scale = 1.0 / jnp.sqrt(jnp.maximum(square, 0.0) + EPSILON)

        def correct(sector, carry):
            one = current[sector]
            value = precondition_ref[sector] * (applied[sector] - rho * one)
            value = (value - correlation * one) * scale
            direction[sector] = value
            low[sector] = value.astype(jnp.bfloat16)
            return carry

        lax.fori_loop(0, sectors, correct, 0)
        operator(1 + iteration, product)
        sums = all_sums(
            2 + 2 * iteration,
            3,
            lambda s: (current[s] * product[s], direction[s] * applied[s], direction[s] * product[s]),
        )
        cross = 0.5 * (sums[0] + sums[1])
        far = sums[2]
        across, along = -2.0 * cross, far - rho
        largest = jnp.maximum(jnp.abs(across), jnp.abs(along))
        still = largest == 0.0
        safe = jnp.where(still, 1.0, largest)
        across, along = across / safe, jnp.where(still, 1.0, along / safe)
        length = jnp.sqrt(across * across + along * along)
        bigger = jnp.sqrt(0.5 * (length + jnp.abs(along)) / length)
        smaller = 0.5 * jnp.abs(across) / (length * bigger)
        ahead = along >= 0.0
        cosine = jnp.where(ahead, bigger, smaller)
        sine = jnp.where(ahead, smaller, bigger)
        sine = jnp.where(across > 0.0, sine, -sine)
        energy = cosine * cosine * rho + 2.0 * cosine * sine * cross + sine * sine * far
        last = iteration == ITERS - 1

        def rotate(sector, carry):
            value = cosine * current[sector] + sine * direction[sector]
            if last:
                state_ref[sector] = value
            else:
                current[sector] = value
                applied[sector] = cosine * applied[sector] + sine * product[sector]
            return carry

        lax.fori_loop(0, sectors, rotate, 0)
    energy_ref[...] = jnp.broadcast_to(energy, energy_ref.shape)


def davidson(tables, live_mask, start, precondition, left_pairs, gate, group_total, capacity):
    pairs = left_pairs.shape[0]
    sectors, rows, columns = start.shape
    sorted_pair, slot_source, from_self, arrived_slot, own_position = tables
    sorted_pair = jnp.concatenate([sorted_pair, sorted_pair // CLASSES])
    arrived_slot = jnp.concatenate([arrived_slot % capacity, arrived_slot // capacity])
    turns = ITERS + 1
    rounds = 2 * ITERS + 1
    others = group_total - 1
    smem = pl.BlockSpec(memory_space=pltpu.SMEM)
    vmem = pl.BlockSpec(memory_space=pltpu.VMEM)
    vector = pltpu.VMEM((sectors, rows, columns), jnp.float32)
    kernel = functools.partial(
        davidson_kernel, group_total, capacity, float(group_total * sectors * rows * columns)
    )
    return pl.pallas_call(
        kernel,
        out_shape=(
            jax.ShapeDtypeStruct(start.shape, jnp.float32),
            jax.ShapeDtypeStruct((8, 128), jnp.float32),
        ),
        in_specs=[smem] * 5 + [vmem] * 4 + [pl.BlockSpec(memory_space=pl.ANY)],
        out_specs=(vmem, vmem),
        scratch_shapes=[
            vector,
            vector,
            vector,
            vector,
            pltpu.VMEM((sectors, rows, columns), jnp.bfloat16),
            pltpu.VMEM((capacity, left_pairs.shape[2], columns), jnp.bfloat16),
            pltpu.VMEM((pairs, rows, columns), jnp.float32),
            pltpu.VMEM((turns, others, capacity, rows, columns), jnp.bfloat16),
            pltpu.VMEM((turns, others, capacity, rows, columns), jnp.bfloat16),
            pltpu.VMEM((rounds, 8, columns // 2), jnp.float32),
            pltpu.VMEM((rounds, group_total, 8, columns // 2), jnp.float32),
            pltpu.SemaphoreType.DMA((turns, others)),
            pltpu.SemaphoreType.DMA((turns, others)),
            pltpu.SemaphoreType.DMA((rounds, others)),
            pltpu.SemaphoreType.DMA((rounds, others)),
            pltpu.VMEM(gate.shape, gate.dtype),
            pltpu.SemaphoreType.DMA((sectors,)),
        ],
        compiler_params=pltpu.CompilerParams(
            collective_id=0, has_side_effects=True, vmem_limit_bytes=58 * 1024 * 1024
        ),
    )(
        sorted_pair,
        slot_source,
        from_self,
        arrived_slot,
        own_position,
        live_mask,
        start,
        precondition,
        left_pairs,
        gate,
    )


def on_device(
    left_environment,
    right_environment,
    site_previous,
    state_start,
    preconditioner,
    channel_tensor,
    channel_mask,
    sector_shift,
    left_sizes,
    right_sizes,
):
    group_total = lax.axis_size("sec")
    my_group = lax.axis_index("sec")
    offset = my_group * SEC_DEV
    capacity = (CLASSES * SEC_DEV + group_total - 1) // group_total
    channel_mix = channel_tensor * channel_mask.astype(jnp.bfloat16)[:, None, :, None]
    live_mask = live_masks(left_sizes, right_sizes, offset)
    own_left = left_environment[0]
    position = lax.axis_index("seg")
    came_right = passed_along(right_environment[0], "seg", -1)
    right_used = jnp.where(position == lax.axis_size("seg") - 1, right_environment[0], came_right)
    gate = build_gate(right_used, channel_mix, 0, SEC_DEV // 2, None)
    fresh, own_pairs, gate = build_environment(
        own_left, site_previous[0], channel_mix, sector_shift, offset, gate
    )
    handed = passed_along(fresh, "seg", 1)
    left_pairs = jnp.where(position == 0, own_pairs, handed)
    gate = build_gate(right_used, channel_mix, SEC_DEV // 2, SEC_DEV, gate)
    tables = routing_tables(sector_shift, my_group, group_total, capacity)
    state, energy = davidson(
        tables, live_mask, state_start[0], preconditioner[0], left_pairs, gate, group_total, capacity
    )
    return (state[None], energy[0, 0:1])


def solution(mesh):
    in_specs = (
        P("seg", "sec", None, None),
        P("seg", "sec", None, None),
        P("seg", "sec", None, None),
        P("seg", "sec", None, None),
        P("seg", "sec", None, None),
        P(),
        P(),
        P(),
        P(),
        P(),
    )
    out_specs = (P("seg", "sec", None, None), P("seg"))
    return jax.shard_map(
        on_device, mesh=mesh, in_specs=in_specs, out_specs=out_specs, check_vma=False
    )
```
